256 devices in a mesh: seq: 16 (over z, x_lo), expert: 8 (over y, core), ffn: 2 (over x_hi).
Axes of the slice: x: 4 (x_hi: 2, x_lo: 2; x = x_hi * 2 + x_lo), y: 4, z: 8, core: 2. Of those that a mesh axis runs over, the one named last changes fastest.
Arguments:
- queries: bfloat16 [2048, 4096], P('seq', ('expert', 'ffn')), may hold values from -122 to 122
- keys: bfloat16 [2048, 1024], P('seq', 'expert'), may hold values from -4.1 to 4.1
- values: bfloat16 [2048, 1024], P('seq', 'expert'), may hold values from -6 to 6
- residual_in: bfloat16 [2048, 4096], P('seq', ('expert', 'ffn')), may hold values from -6 to 6
- routes: int32 [2048, 2], P('seq'), may hold values from 0 to 7, all different within a row; in each aligned block of 128 rows (0 to 127, 128 to 255, ...) at most 48 rows name the same one
- router: bfloat16 [4096, 8], replicated, may hold values from -0.09375 to 0.09375
- w_gate: bfloat16 [8, 4096, 14336], P('expert', None, ('seq', 'ffn')), may hold values from -0.09375 to 0.09375
- w_up: bfloat16 [8, 4096, 14336], P('expert', None, ('seq', 'ffn')), may hold values from -0.09375 to 0.09375
- w_down: bfloat16 [8, 14336, 4096], P('expert', ('seq', 'ffn')), may hold values from -0.046875 to 0.046875
Outputs:
- block_out: bfloat16 [2048, 4096], P('seq', ('expert', 'ffn'))
The draws below stay inside these ranges and needn't reach their ends.
Inputs may be any that keep to these rules, and one draw needn't show every extreme that they name: `routes`: each token names two different experts; among the 128 tokens of one index of seq no expert is named more than 48 times, a bound that some block reaches.
All inputs are finite; a program needn't handle non-finite values.
Results may differ from the reference program's by a relative error of at most 0.0052.
Values may be sent and summed in bfloat16 or wider, within the bound.
No kernel may reach another device: no remote copies, remote signals or barrier semaphores. Data moves between devices by JAX's collectives and lax.ppermute only.
A program may use at most 128 MiB of HBM per device.

```python
import math
import jax
import jax.numpy as jnp
import numpy as np
from jax import lax

D = 4096
HEADS = 32
KV_HEADS = 8
HEAD_DIM = 128
FF = 14336
TOK_SEQ = 128
EXPERTS = 8
TOKENS = 2048
CAP = 48
N_SEQ = 16


def shared_keys(key):
    base = jax.random.truncated_normal(key, -4.0, 4.0, (TOKENS, KV_HEADS * HEAD_DIM), jnp.float32)
    return base


def draw_keys(key, part):
    return shared_keys(key).astype(jnp.bfloat16)


def draw_queries(key, part):
    key = jax.random.fold_in(key, 5)
    return jax.random.truncated_normal(key, -4.0, 4.0, (TOKENS, HEADS * HEAD_DIM), jnp.float32).astype(jnp.bfloat16)


def level_of(stream_key, shape, shards, smallest, high):
    def one(dim, blocks):
        heights = jax.random.uniform(jax.random.fold_in(jax.random.fold_in(stream_key, 6), dim), (blocks,), jnp.float32, smallest / len(shards), high / len(shards))
        return jnp.repeat(jnp.exp(heights), shape[dim] // blocks).reshape((-1,) + (1,) * (len(shape) - dim - 1))

    loudness = one(*shards[0])
    for cut in shards[1:]:
        loudness = loudness * one(*cut)
    return loudness


def deal_out(rng, own, number, rows, amount, top, reach, lean):
    sequence = jax.random.permutation(rng, amount)
    heavy_load, common = load_shares(amount, rows * top, reach, lean, True), load_shares(amount, rows * top, reach, lean, False)
    places = jnp.arange(amount)

    def named(lengths, offset_by):
        used = int((lengths > 0).sum())
        fixed = max(1, used // 4)
        moved = fixed + (places - fixed + offset_by * (used - fixed)) % max(1, amount - fixed)
        return jnp.zeros((amount,), jnp.int32).at[sequence[jnp.where(places < fixed, places, moved)]].set(jnp.asarray(lengths, jnp.int32))

    lengths = jnp.where(number % 4 == 0, named(heavy_load, number // 4), named(common, number - number // 4 - 1))
    mixed = jax.random.permutation(jax.random.fold_in(own, 3), amount)
    source_of, receiver = mixed[0:amount // 2 * 2:2], mixed[1:amount // 2 * 2:2]
    margin = jnp.minimum(lengths[source_of] - 1, reach - lengths[receiver]) // 2
    margin = jnp.where((source_of == sequence[0]) | (receiver == sequence[0]) | (lengths[receiver] == 0), 0, jnp.maximum(margin, 0))
    moved = jax.random.randint(jax.random.fold_in(own, 4), (amount // 2,), 0, 1 << 20) % (margin + 1)
    lengths = lengths.at[source_of].add(-moved).at[receiver].add(moved)
    members = jnp.searchsorted(jnp.cumsum(lengths), jnp.arange(rows * top), side="right").astype(jnp.int32)
    listing = members.reshape(top, rows).T
    listing = listing[jax.random.permutation(jax.random.fold_in(own, 1), rows)]
    offset_by = jax.random.randint(jax.random.fold_in(own, 2), (rows, 1), 0, top)
    return jnp.take_along_axis(listing, (jnp.arange(top)[None, :] + offset_by) % top, axis=1)


def load_shares(number_of, total, limit, lean, full):
    weights = [(1 << 20) // math.isqrt(grade ** lean) + 1 for grade in range(1, number_of + 1)]
    largest = limit if full else min(limit, max(-(-total // number_of), total * weights[0] // sum(weights)))
    least = 1 if total - largest >= number_of - 1 else 0
    holding, spare = [largest] + [least] * (number_of - 1), total - largest - least * (number_of - 1)
    while spare > 0:
        free = [i for i in range(1, number_of) if holding[i] < largest] or [i for i in range(1, number_of) if holding[i] < limit]
        whole, left = sum([weights[i] for i in free]), spare
        for i in free:
            extra = min(limit - holding[i], max(1, left * weights[i] // whole), spare)
            holding[i] = holding[i] + extra
            spare = spare - extra
    return np.array(holding)


def gaussian(rng, dims, scale, bound, shards=(), held_as=jnp.bfloat16):
    values = jax.random.normal(rng, dims, jnp.float32) * scale
    if len(shards) > 0:
        values = level_of(rng, dims, shards, -0.22, 0.18) * values
    return jnp.clip(values, min=-bound, max=bound).astype(held_as)


def setup_inputs(seed: int = 0) -> dict:
    seeds = jax.random.split(jax.random.key(seed), 10)
    queries = draw_queries(jax.random.fold_in(seeds[9], 71), 0)
    keys = draw_keys(jax.random.fold_in(seeds[9], 71), 0)
    values = gaussian(seeds[2], (TOKENS, KV_HEADS * HEAD_DIM), 1.0, 6.0, ((0, 16), (1, 8)))
    residual_in = gaussian(seeds[3], (TOKENS, D), 1.0, 6.0, ((0, 16), (1, 16)))
    routes_keys = jax.random.split(jax.random.fold_in(seeds[4], 1), TOKENS // TOK_SEQ)
    routes_turns = jax.random.permutation(jax.random.fold_in(seeds[4], 3), TOKENS // TOK_SEQ)
    routes = jax.vmap(lambda own, number: deal_out(jax.random.fold_in(seeds[4], 2), own, number, TOK_SEQ, EXPERTS, 2, CAP, 1))(routes_keys, routes_turns).reshape((TOKENS, 2))
    router = gaussian(seeds[5], (D, EXPERTS), D ** -0.5, 0.09375)
    w_gate = gaussian(seeds[6], (EXPERTS, D, FF), D ** -0.5, 0.09375, ((0, 8), (2, 32)))
    w_up = gaussian(seeds[7], (EXPERTS, D, FF), D ** -0.5, 0.09375, ((0, 8), (2, 32)))
    w_down = gaussian(seeds[8], (EXPERTS, FF, D), FF ** -0.5, 0.046875, ((0, 8), (1, 32)))
    return dict(queries=queries, keys=keys, values=values, residual_in=residual_in, routes=routes, router=router, w_gate=w_gate, w_up=w_up, w_down=w_down)


def reference(queries, keys, values, residual_in, routes, router, w_gate, w_up, w_down):
    group = HEADS // KV_HEADS
    q_heads = queries.reshape(TOKENS, HEADS, HEAD_DIM).transpose(1, 0, 2)
    k_heads = jnp.repeat(keys.reshape(TOKENS, KV_HEADS, HEAD_DIM).transpose(1, 0, 2), group, axis=0)
    v_heads = jnp.repeat(values.reshape(TOKENS, KV_HEADS, HEAD_DIM).transpose(1, 0, 2), group, axis=0)
    positions = jnp.arange(TOKENS)
    allowed = positions[None, :] <= positions[:, None]

    def one_head(trio):
        query, key_head, value_head = trio
        scores = jnp.dot(query, key_head.T, preferred_element_type=jnp.float32) * (HEAD_DIM ** -0.5)
        masked = jnp.where(allowed, scores, -jnp.inf)
        top = jnp.max(masked, axis=1, keepdims=True)
        probs = jnp.exp(masked - top)
        weighted = jnp.dot(probs, value_head.astype(jnp.float32), precision=lax.Precision.HIGHEST)
        return weighted / jnp.sum(probs, axis=1, keepdims=True)

    attended = lax.map(one_head, (q_heads, k_heads, v_heads))
    attended = attended.transpose(1, 0, 2).reshape(TOKENS, HEADS * HEAD_DIM)
    mixed32 = residual_in.astype(jnp.float32) + attended
    mixed = mixed32.astype(jnp.bfloat16)
    logits = jnp.dot(mixed, router, preferred_element_type=jnp.float32)
    own = jnp.take_along_axis(logits, routes, axis=1)
    other = jnp.take_along_axis(logits, routes[:, ::-1], axis=1)
    gate = 1.0 / (1.0 + jnp.exp(other - own))
    blocks = routes.reshape(N_SEQ, TOK_SEQ * 2)
    hot = (blocks[..., None] == jnp.arange(EXPERTS)[None, None, :]).astype(jnp.int32)
    slot = jnp.sum((jnp.cumsum(hot, axis=1) - hot) * hot, axis=2).astype(jnp.int32)
    block_id = jnp.broadcast_to(jnp.arange(N_SEQ)[:, None], (N_SEQ, TOK_SEQ * 2)).astype(jnp.int32)
    token_id = (block_id * TOK_SEQ + jnp.arange(TOK_SEQ * 2)[None, :] // 2).astype(jnp.int32)
    tok_of = jnp.full((N_SEQ, EXPERTS, CAP), TOKENS, jnp.int32).at[block_id, blocks, slot].set(token_id)
    gate_of = jnp.zeros((N_SEQ, EXPERTS, CAP), jnp.float32).at[block_id, blocks, slot].set(gate.reshape(N_SEQ, TOK_SEQ * 2))
    padded = jnp.concatenate([mixed, jnp.zeros((1, D), jnp.bfloat16)], axis=0)

    def expert_step(total, pack):
        gate_w, up_w, down_w, toks, gates = pack
        flat_toks = toks.reshape(-1)
        rows = padded[flat_toks]
        gate_val = jnp.dot(rows, gate_w, preferred_element_type=jnp.float32)
        up_val = jnp.dot(rows, up_w, preferred_element_type=jnp.float32)
        hidden = (jax.nn.silu(gate_val) * up_val).astype(jnp.bfloat16)
        result = jnp.dot(hidden, down_w, preferred_element_type=jnp.float32) * gates.reshape(-1)[:, None]
        return total.at[flat_toks].add(result), None

    total, unused = lax.scan(expert_step, jnp.zeros((TOKENS + 1, D), jnp.float32),
                             (w_gate, w_up, w_down, tok_of.transpose(1, 0, 2), gate_of.transpose(1, 0, 2)))
    return (mixed32 + total[:TOKENS]).astype(jnp.bfloat16)
```

```python
import jax
import jax.numpy as jnp
from jax import lax
from jax.sharding import PartitionSpec as P

HEADS = 32
KV_HEADS = 8
HEAD_DIM = 128
NZ, NX = 8, 4
GROUP = ("seq", "ffn")


def place_of(z, x):
    return (z * 2 + x % 2) * 2 + x // 2


def hop(value, dz=0, dx=0):
    pairs = [
        (place_of(z, x), place_of((z + dz) % NZ, (x + dx) % NX))
        for z in range(NZ)
        for x in range(NX)
    ]
    return lax.ppermute(value, GROUP, pairs)


def attention(queries, key_all, value_all, q_pos):
    tok = queries.shape[0]
    heads = queries.shape[1] // HEAD_DIM
    q_heads = queries.reshape(tok, heads, HEAD_DIM)
    scores = jnp.einsum("qhd,kd->hqk", q_heads, key_all, preferred_element_type=jnp.float32)
    scores = scores * HEAD_DIM ** (-0.5)
    allowed = jnp.arange(key_all.shape[0])[None, None, :] <= q_pos[None, :, None]
    masked = jnp.where(allowed, scores, -1e30)
    high = jnp.max(masked, axis=2, keepdims=True)
    probs = jnp.where(allowed, jnp.exp(masked - high), 0.0)
    total = jnp.sum(probs, axis=2, keepdims=True)
    accum = jnp.einsum(
        "hqk,kd->hqd", probs, value_all.astype(jnp.float32), precision=lax.Precision.HIGHEST
    )
    return (accum / total).transpose(1, 0, 2).reshape(tok, heads * HEAD_DIM)


def shards(queries, keys, values, residual_in, routes, router, w_gate, w_up, w_down):
    n_exp = lax.axis_size("expert")
    n_ffn = lax.axis_size("ffn")
    n_seq = lax.axis_size("seq")
    seq_pos = lax.axis_index("seq")
    exp_pos = lax.axis_index("expert")
    ffn_pos = lax.axis_index("ffn")
    tok = queries.shape[0]
    width = router.shape[0]
    span = residual_in.shape[1]
    capacity = 3 * tok // n_exp
    half_cap = capacity // n_ffn
    half = width // 2

    pair = jnp.concatenate([keys, values], axis=1)
    pairs = lax.all_to_all(
        jnp.broadcast_to(pair[None], (n_seq,) + pair.shape), "seq", 0, 0, tiled=True
    ).reshape(n_seq * tok, pair.shape[1])
    key_all, value_all = pairs[:, :HEAD_DIM], pairs[:, HEAD_DIM:]

    flat = routes.reshape(-1)
    partner_flat = routes[:, ::-1].reshape(-1)
    hot = (flat[:, None] == jnp.arange(n_exp)[None, :]).astype(jnp.int32)
    slot = jnp.sum((jnp.cumsum(hot, axis=0) - hot) * hot, axis=1)
    target = flat * capacity + slot
    placed = (jnp.arange(n_exp * capacity)[:, None] == target[None, :]).astype(jnp.int32)
    place_matrix = jnp.sum(placed.reshape(n_exp * capacity, tok, 2), axis=2).astype(jnp.bfloat16)

    q_pos = seq_pos * tok + jnp.arange(tok)
    attended = attention(queries, key_all, value_all, q_pos)
    mixed32 = residual_in.astype(jnp.float32) + attended
    mixed = mixed32.astype(jnp.bfloat16)

    buckets = jnp.dot(place_matrix, mixed, preferred_element_type=jnp.float32).astype(jnp.bfloat16)
    send = buckets.reshape(n_exp * n_ffn, half_cap, 1, span)
    rows = lax.all_to_all(
        send, ("expert", "ffn"), split_axis=0, concat_axis=2, tiled=True
    ).reshape(half_cap, width)

    partner_slots = jnp.sum(placed * partner_flat[None, :], axis=1).reshape(n_exp * n_ffn, half_cap)
    partner = lax.dynamic_slice_in_dim(partner_slots, exp_pos * n_ffn + ffn_pos, 1, 0)[0]
    logits = jnp.dot(rows, router, preferred_element_type=jnp.float32)
    ids = jnp.arange(n_exp)[None, :]
    own = jnp.sum(jnp.where(ids == exp_pos, logits, 0.0), axis=1)
    other = jnp.sum(jnp.where(ids == partner[:, None], logits, 0.0), axis=1)
    weight = 1.0 / (1.0 + jnp.exp(other - own))

    gate_w, up_w, down_w = w_gate[0], w_up[0], w_down[0]

    def dot32(a, b):
        return jnp.dot(a, b, preferred_element_type=jnp.float32)

    def hidden_of(block):
        return (jax.nn.silu(dot32(block, gate_w)) * dot32(block, up_w)).astype(jnp.bfloat16)

    def partial_of(block):
        return dot32(hidden_of(block), down_w)

    block = jnp.concatenate([rows, hop(rows, dx=-1), hop(rows, dx=-2), hop(rows, dx=-3)], axis=0)
    up, down = [block], [block]
    for step in range(1, NZ // 2):
        up.append(hop(up[-1], dz=-1))
        down.append(hop(down[-1], dz=1))
    far = jnp.concatenate([hop(up[-1][:, :half], dz=-1), hop(down[-1][:, half:], dz=1)], axis=1)

    def half_sum(whole, part, left):
        pads = ((0, 0), (0, half)) if left else ((0, 0), (half, 0))
        return whole + jnp.pad(part.astype(jnp.float32), pads)

    partial = partial_of(far).astype(jnp.bfloat16)
    run_up = hop(partial[:, :half], dz=1)
    run_down = hop(partial[:, half:], dz=-1)
    for step in range(NZ // 2 - 1, 0, -1):
        part_up, part_down = partial_of(up[step]), partial_of(down[step])
        if step == NZ // 2 - 1:
            part_up = half_sum(part_up, run_up, True)
            part_down = half_sum(part_down, run_down, False)
        else:
            part_up = part_up + run_up.astype(jnp.float32)
            part_down = part_down + run_down.astype(jnp.float32)
        run_up = hop(part_up.astype(jnp.bfloat16), dz=1)
        run_down = hop(part_down.astype(jnp.bfloat16), dz=-1)
    total = partial_of(block) + run_up.astype(jnp.float32) + run_down.astype(jnp.float32)
    total = total.reshape(NX, half_cap, width)
    sent = total.astype(jnp.bfloat16)
    result = total[0]
    for k in range(1, NX):
        result = result + hop(sent[k], dx=k).astype(jnp.float32)

    back = (result * weight[:, None]).astype(jnp.bfloat16).reshape(half_cap, n_exp * n_ffn, span)
    returned = lax.all_to_all(
        back, ("expert", "ffn"), split_axis=1, concat_axis=0, tiled=True
    ).reshape(n_exp * capacity, span)
    moe = jnp.einsum("st,sd->td", place_matrix, returned, preferred_element_type=jnp.float32)
    return (mixed32 + moe).astype(jnp.bfloat16)


def solution(mesh):
    placed = (
        P("seq", ("expert", "ffn")),
        P("seq", "expert"),
        P("seq", "expert"),
        P("seq", ("expert", "ffn")),
        P("seq", None),
        P(),
        P("expert", None, ("seq", "ffn")),
        P("expert", None, ("seq", "ffn")),
        P("expert", ("seq", "ffn"), None),
    )
    return jax.shard_map(
        shards, mesh=mesh, in_specs=placed, out_specs=P("seq", ("expert", "ffn")), check_vma=False
    )
```

```python
import functools

import jax
import jax.numpy as jnp
from jax import lax
from jax.experimental import pallas as pl
from jax.experimental.pallas import tpu as pltpu
from jax.sharding import PartitionSpec as P

HEADS = 32
KV_HEADS = 8
HEAD_DIM = 128
NZ, NX, NY = 8, 4, 4
ALL = ("seq", "expert", "ffn")


def place_of(z, x, y, core):
    return ((z * 2 + x % 2) * 2 * NY + y * 2 + core) * 2 + x // 2


def hop(value, core_0, core_1):
    pairs = []
    for core, by in enumerate((core_0, core_1)):
        if by is None:
            continue
        dz, dx = by
        for z in range(NZ):
            for x in range(NX):
                for y in range(NY):
                    to = place_of((z + dz) % NZ, (x + dx) % NX, y, core)
                    pairs.append((place_of(z, x, y, core), to))
    return lax.ppermute(value, ALL, pairs)


def expert_kernel(places, outs, tile, *refs):
    pieces = refs[: len(places)]
    gate_ref, up_ref, down_ref = refs[len(places) : len(places) + 3]
    out_refs = refs[len(places) + 3 : len(places) + 3 + len(outs)]
    rows_ref, gate_sum, up_sum, hidden = refs[len(places) + 3 + len(outs) :]
    step = pl.program_id(0)
    steps_in = rows_ref.shape[0]
    across = (((1,), (1,)), ((), ()))

    @pl.when(step == 0)
    def _():
        for (row, col), piece in zip(places, pieces):
            count, width = piece.shape
            for k in range(width // tile):
                rows_ref[col // tile + k, row : row + count, :] = piece[:, k * tile : (k + 1) * tile]
        gate_sum[...] = jnp.zeros_like(gate_sum)
        up_sum[...] = jnp.zeros_like(up_sum)

    @pl.when(step < steps_in)
    def _():
        rows = rows_ref[step]
        gate_sum[...] += lax.dot_general(
            rows, gate_ref[...], across, preferred_element_type=jnp.float32
        )
        up_sum[...] += lax.dot_general(
            rows, up_ref[...], across, preferred_element_type=jnp.float32
        )

    @pl.when(step == steps_in - 1)
    def _():
        value = gate_sum[...]
        hidden[...] = (value / (1.0 + jnp.exp(-value)) * up_sum[...]).astype(jnp.bfloat16)

    for k in range(steps_in):

        @pl.when(step == steps_in + k)
        def _():
            result = jnp.dot(hidden[...], down_ref[...], preferred_element_type=jnp.float32)
            for (row, count, begin, number), out in zip(outs, out_refs):
                if begin <= k < begin + number:
                    out[...] = result[row : row + count]


def expert(groups, gate_t, up_t, down_w, tile=1024):
    units, width = gate_t.shape
    steps = width // tile
    places, outs, arrays, shapes, row = [], [], [], [], 0
    for group in groups:
        col = 0
        for piece in group:
            places.append((row, col))
            outs.append((row, piece.shape[0], col // tile, piece.shape[1] // tile))
            shapes.append(jax.ShapeDtypeStruct(piece.shape, jnp.float32))
            arrays.append(piece)
            col += piece.shape[1]
        row += group[0].shape[0]
    whole = [pl.BlockSpec(p.shape, lambda i: (0, 0)) for p in arrays]
    first = pl.BlockSpec((units, tile), lambda i: (0, jnp.minimum(i, steps - 1)))
    second = pl.BlockSpec((units, tile), lambda i: (0, jnp.maximum(i - steps, 0)))

    def part(begin, number):
        return lambda i: (0, jnp.clip(i - steps - begin, 0, number - 1))

    found = pl.pallas_call(
        functools.partial(expert_kernel, tuple(places), tuple(outs), tile),
        grid=(2 * steps,),
        in_specs=whole + [first, first, second],
        out_specs=[pl.BlockSpec((count, tile), part(b, n)) for _, count, b, n in outs],
        out_shape=shapes,
        scratch_shapes=[
            pltpu.VMEM((steps, row, tile), jnp.bfloat16),
            pltpu.VMEM((row, units), jnp.float32),
            pltpu.VMEM((row, units), jnp.float32),
            pltpu.VMEM((row, units), jnp.bfloat16),
        ],
        compiler_params=pltpu.CompilerParams(vmem_limit_bytes=32 * 1024 * 1024),
        cost_estimate=pl.CostEstimate(
            flops=6 * row * units * width,
            bytes_accessed=6 * units * width + 6 * row * width,
            transcendentals=row * units,
        ),
    )(*arrays, gate_t, up_t, down_w)
    found, results = list(found), []
    for group in groups:
        results.append([found.pop(0) for _ in group])
    return results


def attention(queries, key_all, value_all, q_pos):
    tok = queries.shape[0]
    heads = queries.shape[1] // HEAD_DIM
    q_heads = queries.reshape(tok, heads, HEAD_DIM)
    scores = jnp.einsum("qhd,kd->hqk", q_heads, key_all, preferred_element_type=jnp.float32)
    scores = scores * HEAD_DIM ** (-0.5)
    allowed = jnp.arange(key_all.shape[0])[None, None, :] <= q_pos[None, :, None]
    masked = jnp.where(allowed, scores, -1e30)
    high = jnp.max(masked, axis=2, keepdims=True)
    probs = jnp.where(allowed, jnp.exp(masked - high), 0.0)
    total = jnp.sum(probs, axis=2, keepdims=True)
    accum = jnp.einsum(
        "hqk,kd->hqd", probs, value_all.astype(jnp.float32), precision=lax.Precision.HIGHEST
    )
    return (accum / total).transpose(1, 0, 2).reshape(tok, heads * HEAD_DIM)


def shards(queries, keys, values, residual_in, routes, router, w_gate, w_up, w_down):
    n_exp = lax.axis_size("expert")
    n_ffn = lax.axis_size("ffn")
    n_seq = lax.axis_size("seq")
    seq_pos = lax.axis_index("seq")
    exp_pos = lax.axis_index("expert")
    ffn_pos = lax.axis_index("ffn")
    tok = queries.shape[0]
    width = router.shape[0]
    span = residual_in.shape[1]
    capacity = 3 * tok // n_exp
    half_cap = capacity // n_ffn

    pair = jnp.concatenate([keys, values], axis=1)
    pairs = lax.all_to_all(
        jnp.broadcast_to(pair[None], (n_seq,) + pair.shape), "seq", 0, 0, tiled=True
    ).reshape(n_seq * tok, pair.shape[1])
    key_all, value_all = pairs[:, :HEAD_DIM], pairs[:, HEAD_DIM:]

    flat = routes.reshape(-1)
    partner_flat = routes[:, ::-1].reshape(-1)
    hot = (flat[:, None] == jnp.arange(n_exp)[None, :]).astype(jnp.int32)
    slot = jnp.sum((jnp.cumsum(hot, axis=0) - hot) * hot, axis=1)
    target = flat * capacity + slot
    placed = (jnp.arange(n_exp * capacity)[:, None] == target[None, :]).astype(jnp.int32)
    place_matrix = jnp.sum(placed.reshape(n_exp * capacity, tok, 2), axis=2).astype(jnp.bfloat16)

    q_pos = seq_pos * tok + jnp.arange(tok)
    attended = attention(queries, key_all, value_all, q_pos)
    mixed32 = residual_in.astype(jnp.float32) + attended
    mixed = mixed32.astype(jnp.bfloat16)

    buckets = jnp.dot(place_matrix, mixed, preferred_element_type=jnp.float32).astype(jnp.bfloat16)
    send = buckets.reshape(n_exp * n_ffn, half_cap, 1, span)
    rows = lax.all_to_all(
        send, ("expert", "ffn"), split_axis=0, concat_axis=2, tiled=True
    ).reshape(half_cap, width)

    partner_slots = jnp.sum(placed * partner_flat[None, :], axis=1).reshape(n_exp * n_ffn, half_cap)
    partner = lax.dynamic_slice_in_dim(partner_slots, exp_pos * n_ffn + ffn_pos, 1, 0)[0]
    logits = jnp.dot(rows, router, preferred_element_type=jnp.float32)
    ids = jnp.arange(n_exp)[None, :]
    own = jnp.sum(jnp.where(ids == exp_pos, logits, 0.0), axis=1)
    other = jnp.sum(jnp.where(ids == partner[:, None], logits, 0.0), axis=1)
    weight = 1.0 / (1.0 + jnp.exp(other - own))

    weights = (w_gate[0].T, w_up[0].T, w_down[0])
    zero_core = exp_pos % 2 == 0
    n = half_cap
    block = 4 * n

    def f32(v):
        return v.astype(jnp.float32)

    def b16(v):
        return v.astype(jnp.bfloat16)

    def pick(first, second):
        return jnp.where(zero_core, first, second)

    def pair(sums):
        return [v[0] for v in sums]

    near = [
        hop(rows, (0, -1), (-1, 0)),
        hop(rows, (0, 1), (1, 0)),
        hop(rows, (0, 2), (4, 0)),
    ]
    own = jnp.concatenate([rows] + near, axis=0)
    plus, minus = [None], [None]
    plus.append(hop(own, (-1, 0), (0, -1)))
    minus.append(hop(own, (1, 0), (0, 1)))
    next_plus = hop(own[: 2 * n], None, (-2, 0))
    next_minus = hop(jnp.concatenate([rows, near[1]], axis=0), None, (2, 0))
    other = jnp.concatenate([next_plus, next_minus], axis=0)
    ((sum_own,),) = expert([[own]], *weights)
    sum_own, minus[1] = lax.optimization_barrier((sum_own, minus[1]))
    plus.append(hop(pick(plus[1], other), (-1, 0), (0, -1)))
    minus.append(hop(pick(minus[1], other), (1, 0), (0, 1)))
    sums = {1: pair(expert([[plus[1]], [minus[1]]], *weights))}
    sums[1], minus[2] = lax.optimization_barrier((sums[1], minus[2]))
    plus.append(hop(pick(plus[2], plus[1]), (-1, 0), (0, -1)))
    minus.append(hop(minus[2], (1, 0), (0, 1)))
    sums[2] = pair(expert([[plus[2]], [minus[2]]], *weights))
    sums[2], minus[3] = lax.optimization_barrier((sums[2], minus[3]))
    far_plus = hop(plus[3][: 2 * n], (-1, 0), None)
    far_minus = hop(minus[3][2 * n :], (1, 0), None)
    sums[3] = pair(expert([[plus[3]], [minus[3]]], *weights))
    sums[3], far_minus = lax.optimization_barrier((sums[3], far_minus))
    last = pick(jnp.concatenate([far_plus, far_minus], axis=0), other)
    ((sum_last,),) = expert([[last]], *weights)

    turn_plus = hop(b16(sum_last[: 2 * n]), (1, 0), None)
    turn_minus = hop(b16(sum_last[2 * n :]), (-1, 0), None)
    go_plus = sums[3][0] + jnp.pad(f32(turn_plus), ((0, 2 * n), (0, 0)))
    go_minus = sums[3][1] + jnp.pad(f32(turn_minus), ((2 * n, 0), (0, 0)))
    plus_2, minus_2 = hop(b16(go_plus), (1, 0), (0, 1)), hop(b16(go_minus), (-1, 0), (0, -1))
    go_plus = pick(sums[2][0], sums[1][0]) + f32(plus_2)
    go_minus = sums[2][1] + f32(minus_2)
    plus_3, minus_3 = hop(b16(go_plus), (1, 0), (0, 1)), hop(b16(go_minus), (-1, 0), (0, -1))
    go_plus = pick(sums[1][0] + f32(plus_3), sums[2][0])
    go_minus = sums[1][1] + pick(f32(minus_3), 0.0)
    plus_4, minus_4 = hop(b16(go_plus), (1, 0), (0, 1)), hop(b16(go_minus), (-1, 0), (0, -1))
    total = sum_own + f32(pick(plus_4, plus_3)) + f32(minus_4)
    rest = b16(sum_last + f32(minus_3) + f32(plus_4))
    from_minus, from_plus = hop(rest[: 2 * n], None, (2, 0)), hop(rest[2 * n :], None, (-2, 0))
    chunk = [total[k * n : (k + 1) * n] for k in range(4)]
    chunk_1 = chunk[1] + f32(from_minus[n:])
    chunk_2 = chunk[2] + f32(from_plus[n:])
    result = chunk[0] + f32(from_minus[:n]) + f32(from_plus[:n])
    result = result + f32(hop(b16(chunk[3]), (0, 2), (4, 0)))
    result = result + f32(hop(b16(chunk_1), (0, 1), (1, 0)))
    result = result + f32(hop(b16(chunk_2), (0, -1), (-1, 0)))

    back = (result * weight[:, None]).astype(jnp.bfloat16).reshape(half_cap, n_exp * n_ffn, span)
    returned = lax.all_to_all(
        back, ("expert", "ffn"), split_axis=1, concat_axis=0, tiled=True
    ).reshape(n_exp * capacity, span)
    moe = jnp.einsum("st,sd->td", place_matrix, returned, preferred_element_type=jnp.float32)
    return (mixed32 + moe).astype(jnp.bfloat16)


def solution(mesh):
    placed = (
        P("seq", ("expert", "ffn")),
        P("seq", "expert"),
        P("seq", "expert"),
        P("seq", ("expert", "ffn")),
        P("seq", None),
        P(),
        P("expert", None, ("seq", "ffn")),
        P("expert", None, ("seq", "ffn")),
        P("expert", ("seq", "ffn"), None),
    )
    return jax.shard_map(
        shards, mesh=mesh, in_specs=placed, out_specs=P("seq", ("expert", "ffn")), check_vma=False
    )
```

```python
import functools

import jax
import jax.numpy as jnp
from jax import lax
from jax.experimental import pallas as pl
from jax.experimental.pallas import tpu as pltpu
from jax.sharding import PartitionSpec as P

HEADS = 32
KV_HEADS = 8
HEAD_DIM = 128
NZ, NX, NY = 8, 4, 4
ALL = ("seq", "expert", "ffn")


def place_of(z, x, y, core):
    return ((z * 2 + x % 2) * 2 * NY + y * 2 + core) * 2 + x // 2


def hop(value, core_0, core_1):
    pairs = []
    for core, by in enumerate((core_0, core_1)):
        if by is None:
            continue
        dz, dx = by
        for z in range(NZ):
            for x in range(NX):
                for y in range(NY):
                    to = place_of((z + dz) % NZ, (x + dx) % NX, y, core)
                    pairs.append((place_of(z, x, y, core), to))
    return lax.ppermute(value, ALL, pairs)


def expert_kernel(places, outs, tile, *refs):
    pieces = refs[: len(places)]
    gate_ref, up_ref, down_ref = refs[len(places) : len(places) + 3]
    out_refs = refs[len(places) + 3 : len(places) + 3 + len(outs)]
    rows_ref, gate_sum, up_sum, hidden = refs[len(places) + 3 + len(outs) :]
    step = pl.program_id(0)
    steps_in = rows_ref.shape[0]
    across = (((1,), (1,)), ((), ()))

    @pl.when(step == 0)
    def _():
        for (row, col), piece in zip(places, pieces):
            count, width = piece.shape
            for k in range(width // tile):
                rows_ref[col // tile + k, row : row + count, :] = piece[:, k * tile : (k + 1) * tile]
        gate_sum[...] = jnp.zeros_like(gate_sum)
        up_sum[...] = jnp.zeros_like(up_sum)

    @pl.when(step < steps_in)
    def _():
        rows = rows_ref[step]
        gate_sum[...] += lax.dot_general(
            rows, gate_ref[...], across, preferred_element_type=jnp.float32
        )
        up_sum[...] += lax.dot_general(
            rows, up_ref[...], across, preferred_element_type=jnp.float32
        )

    @pl.when(step == steps_in - 1)
    def _():
        value = gate_sum[...]
        hidden[...] = (value / (1.0 + jnp.exp(-value)) * up_sum[...]).astype(jnp.bfloat16)

    for k in range(steps_in):

        @pl.when(step == steps_in + k)
        def _():
            result = jnp.dot(hidden[...], down_ref[...], preferred_element_type=jnp.float32)
            for (row, count, begin, number), out in zip(outs, out_refs):
                if begin <= k < begin + number:
                    out[...] = result[row : row + count]


def expert(groups, gate_t, up_t, down_w, tile=1024):
    units, width = gate_t.shape
    steps = width // tile
    places, outs, arrays, shapes, row = [], [], [], [], 0
    for group in groups:
        col = 0
        for piece in group:
            places.append((row, col))
            outs.append((row, piece.shape[0], col // tile, piece.shape[1] // tile))
            shapes.append(jax.ShapeDtypeStruct(piece.shape, jnp.float32))
            arrays.append(piece)
            col += piece.shape[1]
        row += group[0].shape[0]
    whole = [pl.BlockSpec(p.shape, lambda i: (0, 0)) for p in arrays]
    first = pl.BlockSpec((units, tile), lambda i: (0, jnp.minimum(i, steps - 1)))
    second = pl.BlockSpec((units, tile), lambda i: (0, jnp.maximum(i - steps, 0)))

    def part(begin, number):
        return lambda i: (0, jnp.clip(i - steps - begin, 0, number - 1))

    found = pl.pallas_call(
        functools.partial(expert_kernel, tuple(places), tuple(outs), tile),
        grid=(2 * steps,),
        in_specs=whole + [first, first, second],
        out_specs=[pl.BlockSpec((count, tile), part(b, n)) for _, count, b, n in outs],
        out_shape=shapes,
        scratch_shapes=[
            pltpu.VMEM((steps, row, tile), jnp.bfloat16),
            pltpu.VMEM((row, units), jnp.float32),
            pltpu.VMEM((row, units), jnp.float32),
            pltpu.VMEM((row, units), jnp.bfloat16),
        ],
        compiler_params=pltpu.CompilerParams(vmem_limit_bytes=32 * 1024 * 1024),
        cost_estimate=pl.CostEstimate(
            flops=6 * row * units * width,
            bytes_accessed=6 * units * width + 6 * row * width,
            transcendentals=row * units,
        ),
    )(*arrays, gate_t, up_t, down_w)
    found, results = list(found), []
    for group in groups:
        results.append([found.pop(0) for _ in group])
    return results


def attention(queries, key_all, value_all, q_pos):
    tok = queries.shape[0]
    heads = queries.shape[1] // HEAD_DIM
    q_heads = queries.reshape(tok, heads, HEAD_DIM)
    scores = jnp.einsum("qhd,kd->hqk", q_heads, key_all, preferred_element_type=jnp.float32)
    scores = scores * HEAD_DIM ** (-0.5)
    allowed = jnp.arange(key_all.shape[0])[None, None, :] <= q_pos[None, :, None]
    masked = jnp.where(allowed, scores, -1e30)
    high = jnp.max(masked, axis=2, keepdims=True)
    probs = jnp.where(allowed, jnp.exp(masked - high), 0.0)
    total = jnp.sum(probs, axis=2, keepdims=True)
    accum = jnp.einsum(
        "hqk,kd->hqd", probs, value_all.astype(jnp.float32), precision=lax.Precision.HIGHEST
    )
    return (accum / total).transpose(1, 0, 2).reshape(tok, heads * HEAD_DIM)


def shards(queries, keys, values, residual_in, routes, router, w_gate, w_up, w_down):
    n_exp = lax.axis_size("expert")
    n_ffn = lax.axis_size("ffn")
    n_seq = lax.axis_size("seq")
    seq_pos = lax.axis_index("seq")
    exp_pos = lax.axis_index("expert")
    ffn_pos = lax.axis_index("ffn")
    tok = queries.shape[0]
    width = router.shape[0]
    span = residual_in.shape[1]
    capacity = 3 * tok // n_exp
    half_cap = capacity // n_ffn

    pair = jnp.concatenate([keys, values], axis=1)
    pairs = lax.all_to_all(
        jnp.broadcast_to(pair[None], (n_seq,) + pair.shape), "seq", 0, 0, tiled=True
    ).reshape(n_seq * tok, pair.shape[1])
    key_all, value_all = pairs[:, :HEAD_DIM], pairs[:, HEAD_DIM:]

    flat = routes.reshape(-1)
    partner_flat = routes[:, ::-1].reshape(-1)
    hot = (flat[:, None] == jnp.arange(n_exp)[None, :]).astype(jnp.int32)
    slot = jnp.sum((jnp.cumsum(hot, axis=0) - hot) * hot, axis=1)
    target = flat * capacity + slot
    placed = (jnp.arange(n_exp * capacity)[:, None] == target[None, :]).astype(jnp.int32)
    place_matrix = jnp.sum(placed.reshape(n_exp * capacity, tok, 2), axis=2).astype(jnp.bfloat16)

    q_pos = seq_pos * tok + jnp.arange(tok)
    attended = attention(queries, key_all, value_all, q_pos)
    mixed32 = residual_in.astype(jnp.float32) + attended
    mixed = mixed32.astype(jnp.bfloat16)

    buckets = jnp.dot(place_matrix, mixed, preferred_element_type=jnp.float32).astype(jnp.bfloat16)
    send = buckets.reshape(n_exp * n_ffn, half_cap, 1, span)
    rows = lax.all_to_all(
        send, ("expert", "ffn"), split_axis=0, concat_axis=2, tiled=True
    ).reshape(half_cap, width)

    partner_slots = jnp.sum(placed * partner_flat[None, :], axis=1).reshape(n_exp * n_ffn, half_cap)
    partner = lax.dynamic_slice_in_dim(partner_slots, exp_pos * n_ffn + ffn_pos, 1, 0)[0]
    logits = jnp.dot(rows, router, preferred_element_type=jnp.float32)
    ids = jnp.arange(n_exp)[None, :]
    own = jnp.sum(jnp.where(ids == exp_pos, logits, 0.0), axis=1)
    other = jnp.sum(jnp.where(ids == partner[:, None], logits, 0.0), axis=1)
    weight = 1.0 / (1.0 + jnp.exp(other - own))

    weights = (w_gate[0].T, w_up[0].T, w_down[0])
    zero_core = exp_pos % 2 == 0
    n = half_cap
    block = 4 * n

    def f32(v):
        return v.astype(jnp.float32)

    def b16(v):
        return v.astype(jnp.bfloat16)

    def pick(first, second):
        return jnp.where(zero_core, first, second)

    def pair(sums):
        return [v[0] for v in sums]

    near = [
        hop(rows, (0, -1), (-1, 0)),
        hop(rows, (0, 1), (1, 0)),
        hop(rows, (0, 2), (-2, 0)),
    ]
    below = hop(rows, None, (2, 0))
    own = jnp.concatenate([rows] + near, axis=0)
    plus, minus = [None], [None]
    plus.append(hop(own, (-1, 0), (0, -1)))
    minus.append(hop(own, (1, 0), (0, 1)))
    wide = [hop(near[2], None, (-1, 0)), hop(below, None, (1, 0)), hop(near[2], None, (-2, 0))]
    other = jnp.concatenate([below] + wide, axis=0)
    ((sum_own,),) = expert([[own]], *weights)
    sum_own, minus[1] = lax.optimization_barrier((sum_own, minus[1]))
    plus.append(hop(pick(plus[1], other), (-1, 0), (0, -1)))
    minus.append(hop(pick(minus[1], other), (1, 0), (0, 1)))
    sums = {1: pair(expert([[plus[1]], [minus[1]]], *weights))}
    sums[1], minus[2] = lax.optimization_barrier((sums[1], minus[2]))
    plus.append(hop(pick(plus[2], plus[1]), (-1, 0), (0, -1)))
    minus.append(hop(minus[2], (1, 0), (0, 1)))
    sums[2] = pair(expert([[plus[2]], [minus[2]]], *weights))
    sums[2], minus[3] = lax.optimization_barrier((sums[2], minus[3]))
    far_plus = hop(plus[3][: 2 * n], (-1, 0), None)
    far_minus = hop(minus[3][2 * n :], (1, 0), None)
    sums[3] = pair(expert([[plus[3]], [minus[3]]], *weights))
    sums[3], far_minus = lax.optimization_barrier((sums[3], far_minus))
    last = pick(jnp.concatenate([far_plus, far_minus], axis=0), other)
    early = hop(b16(pick(sums[3][1], sums[1][1])), (-1, 0), (0, -1))
    ((sum_last,),) = expert([[last]], *weights)

    plus_1, minus_1 = hop(b16(pick(sum_last, sums[3][1])), (1, 0), (0, 1)), early
    go_minus = sums[2][1] + pick(f32(minus_1), 0.0)
    minus_2 = hop(b16(go_minus), (-1, 0), (0, -1))
    go_plus = pick(sums[3][0], sums[2][0]) + f32(plus_1)
    plus_2 = hop(b16(go_plus), (1, 0), (0, 1))
    minus_3 = hop(b16(sums[1][1] + f32(minus_2)), (-1, 0), None)
    plus_3 = hop(b16(pick(sums[2][0] + f32(plus_2), sums[3][0])), (1, 0), (0, 1))
    both = lax.optimization_barrier((plus_2, minus_2))
    rest = sum_last + f32(both[0]) + f32(both[1])
    rest = [rest[k * n : (k + 1) * n] for k in range(4)]
    from_1, from_2 = hop(b16(rest[1]), None, (1, 0)), hop(b16(rest[3]), None, (2, 0))
    from_above = hop(b16(rest[2]), None, (-1, 0))
    from_1, from_2, from_above, _ = lax.optimization_barrier((from_1, from_2, from_above, plus_3))
    plus_4 = hop(b16(sums[1][0] + f32(plus_3)), (1, 0), (0, 1))
    last_down = hop(b16(rest[0] + f32(from_above)), None, (-2, 0))
    last_down, plus_4 = lax.optimization_barrier((last_down, plus_4))
    total = sum_own + f32(plus_4) + f32(pick(minus_3, minus_1))
    chunk = [total[k * n : (k + 1) * n] for k in range(4)]
    result = chunk[0] + f32(last_down)
    result = result + f32(hop(b16(chunk[1]), (0, 1), (1, 0)))
    result = result + f32(hop(b16(chunk[2]), (0, -1), (-1, 0)))
    result = result + f32(hop(b16(chunk[3] + f32(from_1) + f32(from_2)), (0, 2), (2, 0)))

    back = (result * weight[:, None]).astype(jnp.bfloat16).reshape(half_cap, n_exp * n_ffn, span)
    returned = lax.all_to_all(
        back, ("expert", "ffn"), split_axis=1, concat_axis=0, tiled=True
    ).reshape(n_exp * capacity, span)
    moe = jnp.einsum("st,sd->td", place_matrix, returned, preferred_element_type=jnp.float32)
    return (mixed32 + moe).astype(jnp.bfloat16)


def solution(mesh):
    placed = (
        P("seq", ("expert", "ffn")),
        P("seq", "expert"),
        P("seq", "expert"),
        P("seq", ("expert", "ffn")),
        P("seq", None),
        P(),
        P("expert", None, ("seq", "ffn")),
        P("expert", None, ("seq", "ffn")),
        P("expert", ("seq", "ffn"), None),
    )
    return jax.shard_map(
        shards, mesh=mesh, in_specs=placed, out_specs=P("seq", ("expert", "ffn")), check_vma=False
    )
```

```python
import functools

import jax
import jax.numpy as jnp
from jax import lax
from jax.experimental import pallas as pl
from jax.experimental.pallas import tpu as pltpu
from jax.sharding import PartitionSpec as P

HEADS = 32
KV_HEADS = 8
HEAD_DIM = 128
NZ, NX, NY = 8, 4, 4
ALL = ("seq", "expert", "ffn")


def place_of(z, x, y, core):
    return ((z * 2 + x % 2) * 2 * NY + y * 2 + core) * 2 + x // 2


def hop(value, core_0, core_1):
    pairs = []
    for core, by in enumerate((core_0, core_1)):
        if by is None:
            continue
        dz, dx = by
        for z in range(NZ):
            for x in range(NX):
                for y in range(NY):
                    to = place_of((z + dz) % NZ, (x + dx) % NX, y, core)
                    pairs.append((place_of(z, x, y, core), to))
    return lax.ppermute(value, ALL, pairs)


def expert_kernel(places, outs, tile, *refs):
    pieces = refs[: len(places)]
    gate_ref, up_ref, down_ref = refs[len(places) : len(places) + 3]
    out_refs = refs[len(places) + 3 : len(places) + 3 + len(outs)]
    rows_ref, gate_sum, up_sum, hidden = refs[len(places) + 3 + len(outs) :]
    step = pl.program_id(0)
    steps_in = rows_ref.shape[0]
    across = (((1,), (1,)), ((), ()))

    @pl.when(step == 0)
    def _():
        for (row, col), piece in zip(places, pieces):
            count, width = piece.shape
            for k in range(width // tile):
                rows_ref[col // tile + k, row : row + count, :] = piece[:, k * tile : (k + 1) * tile]
        gate_sum[...] = jnp.zeros_like(gate_sum)
        up_sum[...] = jnp.zeros_like(up_sum)

    @pl.when(step < steps_in)
    def _():
        rows = rows_ref[step]
        gate_sum[...] += lax.dot_general(
            rows, gate_ref[...], across, preferred_element_type=jnp.float32
        )
        up_sum[...] += lax.dot_general(
            rows, up_ref[...], across, preferred_element_type=jnp.float32
        )

    @pl.when(step == steps_in - 1)
    def _():
        value = gate_sum[...]
        hidden[...] = (value / (1.0 + jnp.exp(-value)) * up_sum[...]).astype(jnp.bfloat16)

    for k in range(steps_in):

        @pl.when(step == steps_in + k)
        def _():
            result = jnp.dot(hidden[...], down_ref[...], preferred_element_type=jnp.float32)
            for (row, count, begin, number), out in zip(outs, out_refs):
                if begin <= k < begin + number:
                    out[...] = result[row : row + count]


def expert(groups, gate_t, up_t, down_w, tile=1024):
    units, width = gate_t.shape
    steps = width // tile
    places, outs, arrays, shapes, row = [], [], [], [], 0
    for group in groups:
        col = 0
        for piece in group:
            places.append((row, col))
            outs.append((row, piece.shape[0], col // tile, piece.shape[1] // tile))
            shapes.append(jax.ShapeDtypeStruct(piece.shape, jnp.float32))
            arrays.append(piece)
            col += piece.shape[1]
        row += group[0].shape[0]
    whole = [pl.BlockSpec(p.shape, lambda i: (0, 0)) for p in arrays]
    first = pl.BlockSpec((units, tile), lambda i: (0, jnp.minimum(i, steps - 1)))
    second = pl.BlockSpec((units, tile), lambda i: (0, jnp.maximum(i - steps, 0)))

    def part(begin, number):
        return lambda i: (0, jnp.clip(i - steps - begin, 0, number - 1))

    found = pl.pallas_call(
        functools.partial(expert_kernel, tuple(places), tuple(outs), tile),
        grid=(2 * steps,),
        in_specs=whole + [first, first, second],
        out_specs=[pl.BlockSpec((count, tile), part(b, n)) for _, count, b, n in outs],
        out_shape=shapes,
        scratch_shapes=[
            pltpu.VMEM((steps, row, tile), jnp.bfloat16),
            pltpu.VMEM((row, units), jnp.float32),
            pltpu.VMEM((row, units), jnp.float32),
            pltpu.VMEM((row, units), jnp.bfloat16),
        ],
        compiler_params=pltpu.CompilerParams(vmem_limit_bytes=32 * 1024 * 1024),
        cost_estimate=pl.CostEstimate(
            flops=6 * row * units * width,
            bytes_accessed=6 * units * width + 6 * row * width,
            transcendentals=row * units,
        ),
    )(*arrays, gate_t, up_t, down_w)
    found, results = list(found), []
    for group in groups:
        results.append([found.pop(0) for _ in group])
    return results


def attention(queries, key_all, value_all, q_pos):
    tok = queries.shape[0]
    heads = queries.shape[1] // HEAD_DIM
    q_heads = queries.reshape(tok, heads, HEAD_DIM)
    scores = jnp.einsum("qhd,kd->hqk", q_heads, key_all, preferred_element_type=jnp.float32)
    scores = scores * HEAD_DIM ** (-0.5)
    allowed = jnp.arange(key_all.shape[0])[None, None, :] <= q_pos[None, :, None]
    masked = jnp.where(allowed, scores, -1e30)
    high = jnp.max(masked, axis=2, keepdims=True)
    probs = jnp.where(allowed, jnp.exp(masked - high), 0.0)
    total = jnp.sum(probs, axis=2, keepdims=True)
    accum = jnp.einsum(
        "hqk,kd->hqd", probs, value_all.astype(jnp.float32), precision=lax.Precision.HIGHEST
    )
    return (accum / total).transpose(1, 0, 2).reshape(tok, heads * HEAD_DIM)


def shards(queries, keys, values, residual_in, routes, router, w_gate, w_up, w_down):
    n_exp = lax.axis_size("expert")
    n_ffn = lax.axis_size("ffn")
    n_seq = lax.axis_size("seq")
    seq_pos = lax.axis_index("seq")
    exp_pos = lax.axis_index("expert")
    ffn_pos = lax.axis_index("ffn")
    tok = queries.shape[0]
    width = router.shape[0]
    span = residual_in.shape[1]
    capacity = 3 * tok // n_exp
    half_cap = capacity // n_ffn

    pair = jnp.concatenate([keys, values], axis=1)
    pairs = lax.all_to_all(
        jnp.broadcast_to(pair[None], (n_seq,) + pair.shape), "seq", 0, 0, tiled=True
    ).reshape(n_seq * tok, pair.shape[1])
    key_all, value_all = pairs[:, :HEAD_DIM], pairs[:, HEAD_DIM:]

    flat = routes.reshape(-1)
    partner_flat = routes[:, ::-1].reshape(-1)
    hot = (flat[:, None] == jnp.arange(n_exp)[None, :]).astype(jnp.int32)
    slot = jnp.sum((jnp.cumsum(hot, axis=0) - hot) * hot, axis=1)
    target = flat * capacity + slot
    placed = (jnp.arange(n_exp * capacity)[:, None] == target[None, :]).astype(jnp.int32)
    place_matrix = jnp.sum(placed.reshape(n_exp * capacity, tok, 2), axis=2).astype(jnp.bfloat16)

    q_pos = seq_pos * tok + jnp.arange(tok)
    attended = attention(queries, key_all, value_all, q_pos)
    mixed32 = residual_in.astype(jnp.float32) + attended
    mixed = mixed32.astype(jnp.bfloat16)

    buckets = jnp.dot(place_matrix, mixed, preferred_element_type=jnp.float32).astype(jnp.bfloat16)
    send = buckets.reshape(n_exp * n_ffn, half_cap, 1, span)
    rows = lax.all_to_all(
        send, ("expert", "ffn"), split_axis=0, concat_axis=2, tiled=True
    ).reshape(half_cap, width)

    partner_slots = jnp.sum(placed * partner_flat[None, :], axis=1).reshape(n_exp * n_ffn, half_cap)
    partner = lax.dynamic_slice_in_dim(partner_slots, exp_pos * n_ffn + ffn_pos, 1, 0)[0]
    logits = jnp.dot(rows, router, preferred_element_type=jnp.float32)
    ids = jnp.arange(n_exp)[None, :]
    own = jnp.sum(jnp.where(ids == exp_pos, logits, 0.0), axis=1)
    other = jnp.sum(jnp.where(ids == partner[:, None], logits, 0.0), axis=1)
    weight = 1.0 / (1.0 + jnp.exp(other - own))

    weights = (w_gate[0].T, w_up[0].T, w_down[0])
    zero_core = exp_pos % 2 == 0
    n = half_cap
    block = 4 * n

    def f32(v):
        return v.astype(jnp.float32)

    def b16(v):
        return v.astype(jnp.bfloat16)

    def pick(first, second):
        return jnp.where(zero_core, first, second)

    def pair(sums):
        return [v[0] for v in sums]

    near = [
        hop(rows, (0, -1), (-1, 0)),
        hop(rows, (0, 1), (1, 0)),
        hop(rows, (0, 2), (-2, 0)),
    ]
    below = hop(rows, None, (2, 0))
    own = jnp.concatenate([rows] + near, axis=0)
    plus, minus = [None], [None]
    plus.append(hop(own, (-1, 0), (0, -1)))
    minus.append(hop(own, (1, 0), (0, 1)))
    wide = [hop(near[2], None, (-1, 0)), hop(below, None, (1, 0)), hop(near[2], None, (-2, 0))]
    other = jnp.concatenate([below] + wide, axis=0)
    ((sum_own,),) = expert([[own]], *weights)
    sum_own, minus[1] = lax.optimization_barrier((sum_own, minus[1]))
    plus.append(hop(pick(plus[1], other), (-1, 0), (0, -1)))
    minus.append(hop(pick(minus[1], other), (1, 0), (0, 1)))
    sums = {1: pair(expert([[plus[1]], [minus[1]]], *weights))}
    sums[1], minus[2] = lax.optimization_barrier((sums[1], minus[2]))
    plus.append(hop(pick(plus[2], plus[1]), (-1, 0), (0, -1)))
    minus.append(hop(minus[2], (1, 0), (0, 1)))
    sums[2] = pair(expert([[plus[2]], [minus[2]]], *weights))
    sums[2], minus[3] = lax.optimization_barrier((sums[2], minus[3]))
    far_plus = hop(plus[3][: 2 * n], (-1, 0), None)
    far_minus = hop(minus[3][2 * n :], (1, 0), None)
    sums[3] = pair(expert([[plus[3]], [minus[3]]], *weights))
    sums[3], far_minus = lax.optimization_barrier((sums[3], far_minus))
    last = pick(jnp.concatenate([far_plus, far_minus], axis=0), other)
    early = hop(b16(pick(sums[3][1], sums[1][1])), (-1, 0), (0, -1))
    ((sum_last,),) = expert([[last]], *weights)

    plus_1, minus_1 = hop(b16(pick(sum_last, sums[3][1])), (1, 0), (0, 1)), early
    go_minus = sums[2][1] + pick(f32(minus_1), 0.0)
    minus_2 = hop(b16(go_minus), (-1, 0), (0, -1))
    go_plus = pick(sums[3][0], sums[2][0]) + f32(plus_1)
    plus_2 = hop(b16(go_plus), (1, 0), (0, 1))
    minus_3 = hop(b16(sums[1][1] + f32(minus_2)), (-1, 0), None)
    plus_3 = hop(b16(pick(sums[2][0] + f32(plus_2), sums[3][0])), (1, 0), (0, 1))
    both = lax.optimization_barrier((plus_2, minus_2))
    rest = sum_last + f32(both[0]) + f32(both[1])
    rest = [rest[k * n : (k + 1) * n] for k in range(4)]
    from_1, from_2 = hop(b16(rest[1]), None, (1, 0)), hop(b16(rest[3]), None, (-2, 0))
    from_above = hop(b16(rest[2]), None, (-1, 0))
    from_1, from_2, from_above, _ = lax.optimization_barrier((from_1, from_2, from_above, plus_3))
    plus_4 = hop(b16(sums[1][0] + f32(plus_3)), (1, 0), (0, 1))
    last_down = hop(b16(rest[0] + f32(from_above) + f32(from_2)), None, (-2, 0))
    last_down, plus_4 = lax.optimization_barrier((last_down, plus_4))
    total = sum_own + f32(plus_4) + f32(pick(minus_3, minus_1))
    chunk = [total[k * n : (k + 1) * n] for k in range(4)]
    result = chunk[0] + f32(last_down)
    result = result + f32(hop(b16(chunk[1]), (0, 1), (1, 0)))
    result = result + f32(hop(b16(chunk[2]), (0, -1), (-1, 0)))
    result = result + f32(hop(b16(chunk[3] + f32(from_1)), (0, 2), (2, 0)))

    back = (result * weight[:, None]).astype(jnp.bfloat16).reshape(half_cap, n_exp * n_ffn, span)
    returned = lax.all_to_all(
        back, ("expert", "ffn"), split_axis=1, concat_axis=0, tiled=True
    ).reshape(n_exp * capacity, span)
    moe = jnp.einsum("st,sd->td", place_matrix, returned, preferred_element_type=jnp.float32)
    return (mixed32 + moe).astype(jnp.bfloat16)


def solution(mesh):
    placed = (
        P("seq", ("expert", "ffn")),
        P("seq", "expert"),
        P("seq", "expert"),
        P("seq", ("expert", "ffn")),
        P("seq", None),
        P(),
        P("expert", None, ("seq", "ffn")),
        P("expert", None, ("seq", "ffn")),
        P("expert", ("seq", "ffn"), None),
    )
    return jax.shard_map(
        shards, mesh=mesh, in_specs=placed, out_specs=P("seq", ("expert", "ffn")), check_vma=False
    )
```

```python
import functools

import jax
import jax.numpy as jnp
from jax import lax
from jax.experimental import pallas as pl
from jax.experimental.pallas import tpu as pltpu
from jax.sharding import PartitionSpec as P

HEADS = 32
KV_HEADS = 8
HEAD_DIM = 128
NZ, NX, NY = 8, 4, 4
ALL = ("seq", "expert", "ffn")


def place_of(z, x, y, core):
    return ((z * 2 + x % 2) * 2 * NY + y * 2 + core) * 2 + x // 2


def hop(value, core_0, core_1):
    pairs = []
    for core, by in enumerate((core_0, core_1)):
        if by is None:
            continue
        dz, dx = by
        for z in range(NZ):
            for x in range(NX):
                for y in range(NY):
                    to = place_of((z + dz) % NZ, (x + dx) % NX, y, core)
                    pairs.append((place_of(z, x, y, core), to))
    return lax.ppermute(value, ALL, pairs)


def expert_kernel(places, outs, tile, *refs):
    pieces = refs[: len(places)]
    gate_ref, up_ref, down_ref = refs[len(places) : len(places) + 3]
    out_refs = refs[len(places) + 3 : len(places) + 3 + len(outs)]
    rows_ref, gate_sum, up_sum, hidden = refs[len(places) + 3 + len(outs) :]
    step = pl.program_id(0)
    steps_in = rows_ref.shape[0]
    across = (((1,), (1,)), ((), ()))

    @pl.when(step == 0)
    def _():
        for (row, col), piece in zip(places, pieces):
            count, width = piece.shape
            for k in range(width // tile):
                rows_ref[col // tile + k, row : row + count, :] = piece[:, k * tile : (k + 1) * tile]
        gate_sum[...] = jnp.zeros_like(gate_sum)
        up_sum[...] = jnp.zeros_like(up_sum)

    @pl.when(step < steps_in)
    def _():
        rows = rows_ref[step]
        gate_sum[...] += lax.dot_general(
            rows, gate_ref[...], across, preferred_element_type=jnp.float32
        )
        up_sum[...] += lax.dot_general(
            rows, up_ref[...], across, preferred_element_type=jnp.float32
        )

    @pl.when(step == steps_in - 1)
    def _():
        value = gate_sum[...]
        hidden[...] = (value / (1.0 + jnp.exp(-value)) * up_sum[...]).astype(jnp.bfloat16)

    for k in range(steps_in):

        @pl.when(step == steps_in + k)
        def _():
            result = jnp.dot(hidden[...], down_ref[...], preferred_element_type=jnp.float32)
            for (row, count, begin, number), out in zip(outs, out_refs):
                if begin <= k < begin + number:
                    out[...] = result[row : row + count]


def expert(groups, gate_t, up_t, down_w, tile=1024):
    units, width = gate_t.shape
    steps = width // tile
    places, outs, arrays, shapes, row = [], [], [], [], 0
    for group in groups:
        col = 0
        for piece in group:
            places.append((row, col))
            outs.append((row, piece.shape[0], col // tile, piece.shape[1] // tile))
            shapes.append(jax.ShapeDtypeStruct(piece.shape, jnp.float32))
            arrays.append(piece)
            col += piece.shape[1]
        row += group[0].shape[0]
    whole = [pl.BlockSpec(p.shape, lambda i: (0, 0)) for p in arrays]
    first = pl.BlockSpec((units, tile), lambda i: (0, jnp.minimum(i, steps - 1)))
    second = pl.BlockSpec((units, tile), lambda i: (0, jnp.maximum(i - steps, 0)))

    def part(begin, number):
        return lambda i: (0, jnp.clip(i - steps - begin, 0, number - 1))

    found = pl.pallas_call(
        functools.partial(expert_kernel, tuple(places), tuple(outs), tile),
        grid=(2 * steps,),
        in_specs=whole + [first, first, second],
        out_specs=[pl.BlockSpec((count, tile), part(b, n)) for _, count, b, n in outs],
        out_shape=shapes,
        scratch_shapes=[
            pltpu.VMEM((steps, row, tile), jnp.bfloat16),
            pltpu.VMEM((row, units), jnp.float32),
            pltpu.VMEM((row, units), jnp.float32),
            pltpu.VMEM((row, units), jnp.bfloat16),
        ],
        compiler_params=pltpu.CompilerParams(vmem_limit_bytes=32 * 1024 * 1024),
        cost_estimate=pl.CostEstimate(
            flops=6 * row * units * width,
            bytes_accessed=6 * units * width + 6 * row * width,
            transcendentals=row * units,
        ),
    )(*arrays, gate_t, up_t, down_w)
    found, results = list(found), []
    for group in groups:
        results.append([found.pop(0) for _ in group])
    return results


def attention(queries, key_all, value_all, q_pos):
    tok = queries.shape[0]
    heads = queries.shape[1] // HEAD_DIM
    q_heads = queries.reshape(tok, heads, HEAD_DIM)
    scores = jnp.einsum("qhd,kd->hqk", q_heads, key_all, preferred_element_type=jnp.float32)
    scores = scores * HEAD_DIM ** (-0.5)
    allowed = jnp.arange(key_all.shape[0])[None, None, :] <= q_pos[None, :, None]
    masked = jnp.where(allowed, scores, -1e30)
    high = jnp.max(masked, axis=2, keepdims=True)
    probs = jnp.where(allowed, jnp.exp(masked - high), 0.0)
    total = jnp.sum(probs, axis=2, keepdims=True)
    accum = jnp.einsum(
        "hqk,kd->hqd", probs, value_all.astype(jnp.float32), precision=lax.Precision.HIGHEST
    )
    return (accum / total).transpose(1, 0, 2).reshape(tok, heads * HEAD_DIM)


def shards(queries, keys, values, residual_in, routes, router, w_gate, w_up, w_down):
    n_exp = lax.axis_size("expert")
    n_ffn = lax.axis_size("ffn")
    n_seq = lax.axis_size("seq")
    seq_pos = lax.axis_index("seq")
    exp_pos = lax.axis_index("expert")
    ffn_pos = lax.axis_index("ffn")
    tok = queries.shape[0]
    width = router.shape[0]
    span = residual_in.shape[1]
    capacity = 3 * tok // n_exp
    half_cap = capacity // n_ffn

    pair = jnp.concatenate([keys, values], axis=1)
    pairs = lax.all_to_all(
        jnp.broadcast_to(pair[None], (n_seq,) + pair.shape), "seq", 0, 0, tiled=True
    ).reshape(n_seq * tok, pair.shape[1])
    key_all, value_all = pairs[:, :HEAD_DIM], pairs[:, HEAD_DIM:]

    flat = routes.reshape(-1)
    partner_flat = routes[:, ::-1].reshape(-1)
    hot = (flat[:, None] == jnp.arange(n_exp)[None, :]).astype(jnp.int32)
    slot = jnp.sum((jnp.cumsum(hot, axis=0) - hot) * hot, axis=1)
    target = flat * capacity + slot
    placed = (jnp.arange(n_exp * capacity)[:, None] == target[None, :]).astype(jnp.int32)
    place_matrix = jnp.sum(placed.reshape(n_exp * capacity, tok, 2), axis=2).astype(jnp.bfloat16)

    q_pos = seq_pos * tok + jnp.arange(tok)
    attended = attention(queries, key_all, value_all, q_pos)
    mixed32 = residual_in.astype(jnp.float32) + attended
    mixed = mixed32.astype(jnp.bfloat16)

    buckets = jnp.dot(place_matrix, mixed, preferred_element_type=jnp.float32).astype(jnp.bfloat16)
    send = buckets.reshape(n_exp * n_ffn, half_cap, 1, span)
    rows = lax.all_to_all(
        send, ("expert", "ffn"), split_axis=0, concat_axis=2, tiled=True
    ).reshape(half_cap, width)

    partner_slots = jnp.sum(placed * partner_flat[None, :], axis=1).reshape(n_exp * n_ffn, half_cap)
    partner = lax.dynamic_slice_in_dim(partner_slots, exp_pos * n_ffn + ffn_pos, 1, 0)[0]
    logits = jnp.dot(rows, router, preferred_element_type=jnp.float32)
    ids = jnp.arange(n_exp)[None, :]
    own = jnp.sum(jnp.where(ids == exp_pos, logits, 0.0), axis=1)
    other = jnp.sum(jnp.where(ids == partner[:, None], logits, 0.0), axis=1)
    weight = 1.0 / (1.0 + jnp.exp(other - own))

    weights = (w_gate[0].T, w_up[0].T, w_down[0])
    zero_core = exp_pos % 2 == 0
    n = half_cap
    block = 4 * n

    def f32(v):
        return v.astype(jnp.float32)

    def b16(v):
        return v.astype(jnp.bfloat16)

    def pick(first, second):
        return jnp.where(zero_core, first, second)

    def pair(sums):
        return [v[0] for v in sums]

    near = [
        hop(rows, (0, -1), (-1, 0)),
        hop(rows, (0, 1), (1, 0)),
        hop(rows, (0, 2), (-2, 0)),
    ]
    below = hop(rows, None, (2, 0))
    own = jnp.concatenate([rows] + near, axis=0)
    plus, minus = [None], [None]
    plus.append(hop(own, (-1, 0), (0, -1)))
    minus.append(hop(own, (1, 0), (0, 1)))
    wide = [hop(near[2], None, (-1, 0)), hop(below, None, (1, 0)), hop(near[2], None, (-2, 0))]
    other = jnp.concatenate([below] + wide, axis=0)
    ((sum_own,),) = expert([[own]], *weights)
    sum_own, minus[1] = lax.optimization_barrier((sum_own, minus[1]))
    plus.append(hop(pick(plus[1], other), (-1, 0), (0, -1)))
    minus.append(hop(pick(minus[1], other), (1, 0), (0, 1)))
    sums = {1: pair(expert([[plus[1]], [minus[1]]], *weights))}
    sums[1], minus[2] = lax.optimization_barrier((sums[1], minus[2]))
    plus.append(hop(pick(plus[2], plus[1]), (-1, 0), (0, -1)))
    minus.append(hop(minus[2], (1, 0), (0, 1)))
    sums[2] = pair(expert([[plus[2]], [minus[2]]], *weights))
    sums[2], minus[3] = lax.optimization_barrier((sums[2], minus[3]))
    far_plus = hop(plus[3][: 2 * n], (-1, 0), None)
    far_minus = hop(minus[3][2 * n :], (1, 0), None)
    sums[3] = pair(expert([[plus[3]], [minus[3]]], *weights))
    sums[3], far_minus = lax.optimization_barrier((sums[3], far_minus))
    last = pick(jnp.concatenate([far_plus, far_minus], axis=0), other)
    early = hop(b16(pick(sums[3][1], sums[1][1])), (-1, 0), (0, -1))
    ((sum_last,),) = expert([[last]], *weights)

    plus_1, minus_1 = hop(b16(pick(sum_last, sums[3][1])), (1, 0), (0, 1)), early
    go_minus = sums[2][1] + pick(f32(minus_1), 0.0)
    minus_2 = hop(b16(go_minus), (-1, 0), (0, -1))
    go_plus = pick(sums[3][0], sums[2][0]) + f32(plus_1)
    plus_2 = hop(b16(go_plus), (1, 0), (0, 1))
    minus_3 = hop(b16(sums[1][1] + f32(minus_2)), (-1, 0), None)
    plus_3 = hop(b16(pick(sums[2][0] + f32(plus_2), sums[3][0])), (1, 0), (0, 1))
    both = lax.optimization_barrier((plus_2, minus_2, plus_3))
    rest = sum_last + f32(both[0]) + f32(both[1])
    rest = [rest[k * n : (k + 1) * n] for k in range(4)]
    from_1, from_2 = hop(b16(rest[1]), None, (1, 0)), hop(b16(rest[3]), None, (-2, 0))
    from_above = hop(b16(rest[2]), None, (-1, 0))
    plus_4 = hop(b16(sums[1][0] + f32(plus_3)), (1, 0), (0, 1))
    from_1, from_2, from_above, plus_4 = lax.optimization_barrier(
        (from_1, from_2, from_above, plus_4)
    )
    last_down = hop(b16(rest[0] + f32(from_above) + f32(from_2)), None, (-2, 0))
    total = sum_own + f32(plus_4) + f32(pick(minus_3, minus_1))
    chunk = [total[k * n : (k + 1) * n] for k in range(4)]
    result = chunk[0] + f32(last_down)
    result = result + f32(hop(b16(chunk[1]), (0, 1), (1, 0)))
    result = result + f32(hop(b16(chunk[2]), (0, -1), (-1, 0)))
    result = result + f32(hop(b16(chunk[3] + f32(from_1)), (0, 2), (2, 0)))

    back = (result * weight[:, None]).astype(jnp.bfloat16).reshape(half_cap, n_exp * n_ffn, span)
    returned = lax.all_to_all(
        back, ("expert", "ffn"), split_axis=1, concat_axis=0, tiled=True
    ).reshape(n_exp * capacity, span)
    moe = jnp.einsum("st,sd->td", place_matrix, returned, preferred_element_type=jnp.float32)
    return (mixed32 + moe).astype(jnp.bfloat16)


def solution(mesh):
    placed = (
        P("seq", ("expert", "ffn")),
        P("seq", "expert"),
        P("seq", "expert"),
        P("seq", ("expert", "ffn")),
        P("seq", None),
        P(),
        P("expert", None, ("seq", "ffn")),
        P("expert", None, ("seq", "ffn")),
        P("expert", ("seq", "ffn"), None),
    )
    return jax.shard_map(
        shards, mesh=mesh, in_specs=placed, out_specs=P("seq", ("expert", "ffn")), check_vma=False
    )
```
